32 devices in a mesh: prow: 4 (over x, core), pcol: 8 (over z, y).
Axes of the slice: x: 2, y: 2, z: 4, core: 2. Of those that a mesh axis runs over, the one named last changes fastest.
Arguments:
- velocity_u: bfloat16 [128, 1024, 1024], P('prow', 'pcol'), may hold values from -6 to 6
- velocity_v: bfloat16 [128, 1024, 1024], P('prow', 'pcol'), may hold values from -6 to 6
- velocity_w: bfloat16 [128, 1024, 1024], P('prow', 'pcol'), may hold values from -6 to 6
- x_derivative: bfloat16 [1024, 1024], P('pcol'), may hold values from -2 to 2
- y_derivative: bfloat16 [128, 128], replicated, may hold values from -2 to 2
- z_derivative: bfloat16 [1024, 1024], P('prow'), may hold values from -2 to 2
Outputs:
- u_tendency: float32 [128, 1024, 1024], P('pcol', 'prow')
- divergence: float32 [1024, 1024, 128], P('pcol', 'prow')
The draws below stay inside these ranges and needn't reach their ends.
All inputs are finite; a program needn't handle non-finite values.
Results may differ from the reference program's by a relative error of at most 0.0018.
Values may be sent and summed in bfloat16 or wider, within the bound.
A program may use at most 256 MiB of HBM per device.

```python
import math
import jax
import jax.numpy as jnp
from jax import lax

NX = 1024
NY = 128
NZ = 1024
N_PCOL = 8


def operator_draw(key, order, periodic, stretched):
    row_index = jnp.arange(order)[:, None]
    col_index = jnp.arange(order)[None, :]
    offset = col_index - row_index
    if periodic:
        offset = (offset + order // 2) % order - order // 2
    distance = jnp.abs(offset)
    sign_of = jnp.sign(offset).astype(jnp.float32)
    coefficient = jnp.where(distance == 1, 0.75, jnp.where(distance == 2, -0.15, jnp.where(distance == 3, 1.0 / 60.0, 0.0)))
    banded = sign_of * coefficient
    first_key, second_key = jax.random.split(key)
    random_part = jnp.clip(jax.random.normal(first_key, (order, order), jnp.float32), -4.0, 4.0)
    combined = banded + 0.4 / math.sqrt(order) * random_part
    if stretched:
        metric = jnp.exp(jax.random.uniform(second_key, (order, 1), jnp.float32, math.log(0.5), math.log(2.0)))
        combined = combined * metric
    return combined.astype(jnp.bfloat16)


def draw_x_derivative(key, part):
    return operator_draw(jax.random.fold_in(key, 11), NX, True, False)


def draw_y_derivative(key, part):
    return operator_draw(jax.random.fold_in(key, 12), NY, False, True)


def draw_z_derivative(key, part):
    return operator_draw(jax.random.fold_in(key, 13), NZ, True, False)


def shard_levels(own_key, extent, cuts, smallest, high):
    def one(axis_at, shards_of):
        draws = jax.random.uniform(jax.random.fold_in(jax.random.fold_in(own_key, 6), axis_at), (shards_of,), jnp.float32, smallest / len(cuts), high / len(cuts))
        return jnp.repeat(jnp.exp(draws), extent[axis_at] // shards_of).reshape((-1,) + (1,) * (len(extent) - axis_at - 1))

    level = one(*cuts[0])
    for cut in cuts[1:]:
        level = level * one(*cut)
    return level


def noise(stream_key, dims, width, limit, pieces=(), kind=jnp.bfloat16):
    result = jax.random.normal(stream_key, dims, jnp.float32) * width
    if len(pieces) > 0:
        result = shard_levels(stream_key, dims, pieces, -0.22, 0.18) * result
    return jnp.clip(result, min=-limit, max=limit).astype(kind)


def setup_inputs(seed: int = 0) -> dict:
    splits = jax.random.split(jax.random.key(seed), 7)
    velocity_u = noise(splits[0], (NY, NZ, NX), 1.0, 6.0, ((0, 4), (1, 8)))
    velocity_v = noise(splits[1], (NY, NZ, NX), 1.0, 6.0, ((0, 4), (1, 8)))
    velocity_w = noise(splits[2], (NY, NZ, NX), 1.0, 6.0, ((0, 4), (1, 8)))
    x_derivative = draw_x_derivative(jax.random.fold_in(splits[6], 71), 0)
    y_derivative = draw_y_derivative(jax.random.fold_in(splits[6], 71), 0)
    z_derivative = draw_z_derivative(jax.random.fold_in(splits[6], 71), 0)
    return dict(velocity_u=velocity_u, velocity_v=velocity_v, velocity_w=velocity_w, x_derivative=x_derivative, y_derivative=y_derivative, z_derivative=z_derivative)


def reference(velocity_u, velocity_v, velocity_w, x_derivative, y_derivative, z_derivative):
    block_count = N_PCOL
    block_width = NZ // block_count

    def plane_section(index):
        start = (index * block_width).astype(jnp.int32)
        u_part = lax.dynamic_slice_in_dim(velocity_u, start, block_width, 1)
        v_part = lax.dynamic_slice_in_dim(velocity_v, start, block_width, 1)
        u_dx = jnp.dot(u_part.reshape(NY * block_width, NX), x_derivative.T,
                       preferred_element_type=jnp.float32).reshape(NY, block_width, NX).astype(jnp.bfloat16)
        u_dy = jnp.dot(y_derivative, u_part.reshape(NY, block_width * NX),
                       preferred_element_type=jnp.float32).reshape(NY, block_width, NX)
        v_dy = jnp.dot(y_derivative, v_part.reshape(NY, block_width * NX),
                       preferred_element_type=jnp.float32).reshape(NY, block_width, NX)
        partial_div = u_dx.astype(jnp.float32) + v_dy
        advect = u_part.astype(jnp.float32) * u_dx.astype(jnp.float32) + v_part.astype(jnp.float32) * u_dy
        return partial_div, advect

    partial_div, advect = lax.map(plane_section, jnp.arange(block_count, dtype=jnp.int32))
    partial_div = jnp.transpose(partial_div, (1, 0, 2, 3)).reshape(NY, NZ, NX)
    advect = jnp.transpose(advect, (1, 0, 2, 3)).reshape(NY, NZ, NX)

    def line_section(index):
        u_plane = lax.dynamic_index_in_dim(velocity_u, index, 0, keepdims=False)
        w_plane = lax.dynamic_index_in_dim(velocity_w, index, 0, keepdims=False)
        part_plane = lax.dynamic_index_in_dim(partial_div, index, 0, keepdims=False)
        adv_plane = lax.dynamic_index_in_dim(advect, index, 0, keepdims=False)
        u_dz = jnp.dot(z_derivative, u_plane, preferred_element_type=jnp.float32)
        w_dz = jnp.dot(z_derivative, w_plane, preferred_element_type=jnp.float32)
        return part_plane + w_dz, -(adv_plane + w_plane.astype(jnp.float32) * u_dz)

    divergence, u_tendency = lax.map(line_section, jnp.arange(NY, dtype=jnp.int32))
    return jnp.transpose(u_tendency, (0, 2, 1)), jnp.transpose(divergence, (1, 2, 0))
```

```python
import functools
import jax
import jax.numpy as jnp
from jax import lax
from jax.experimental import pallas as pl
from jax.experimental.pallas import tpu as pltpu
from jax.sharding import PartitionSpec as P

F32 = jnp.float32
BF16 = jnp.bfloat16
MIB = 1 << 20


def turn_kernel(rows, *refs):
    count = (len(refs) - 3) // 2
    srcs, dsts = refs[:count], refs[count:2 * count]
    send_sem, recv_sem, own_sem = refs[2 * count:]
    me = lax.axis_index("prow")
    barrier = pltpu.get_barrier_semaphore()
    for k in range(1, rows):
        pl.semaphore_signal(
            barrier, inc=1, device_id={"prow": lax.rem(me + k, rows)}, device_id_type=pl.DeviceIdType.MESH
        )
    pl.semaphore_wait(barrier, rows - 1)

    copies = []
    for n, (src, dst) in enumerate(zip(srcs, dsts)):
        width = dst.shape[-1]

        def columns(q):
            return src.at[:, :, pl.ds(pl.multiple_of(q * width, width), width)]

        for k in range(1, rows):
            q = lax.rem(me + k, rows)
            copy = pltpu.make_async_remote_copy(
                src_ref=columns(q),
                dst_ref=dst.at[me],
                send_sem=send_sem.at[n, k],
                recv_sem=recv_sem.at[n, k],
                device_id={"prow": q},
                device_id_type=pl.DeviceIdType.MESH,
            )
            copy.start()
            copies.append(copy)
        own = pltpu.make_async_copy(columns(me), dst.at[me], own_sem.at[n])
        own.start()
        copies.append(own)
    for copy in copies:
        copy.wait()


def turn(arrays, rows, number):
    y, z, x = arrays[0].shape
    width = x // rows
    if width % 128:
        sent = [a.reshape(y, z, rows, width).transpose(2, 0, 1, 3) for a in arrays]
        return [lax.all_to_all(a, "prow", 0, 0, tiled=True).reshape(rows * y, z, width) for a in sent]
    count = len(arrays)
    outs = pl.pallas_call(
        functools.partial(turn_kernel, rows),
        out_shape=[jax.ShapeDtypeStruct((rows, y, z, width), a.dtype) for a in arrays],
        in_specs=[pl.BlockSpec(memory_space=pl.ANY)] * count,
        out_specs=[pl.BlockSpec(memory_space=pl.ANY)] * count,
        scratch_shapes=[
            pltpu.SemaphoreType.DMA((count, rows)),
            pltpu.SemaphoreType.DMA((count, rows)),
            pltpu.SemaphoreType.DMA((count,)),
        ],
        compiler_params=pltpu.CompilerParams(collective_id=number, has_side_effects=True),
        cost_estimate=pl.CostEstimate(flops=0, bytes_accessed=250 * MIB * count, transcendentals=0),
        name=f"turn_{number}",
    )(*arrays)
    return [out.reshape(rows * y, z, width) for out in outs]


def exchange(array):
    return lax.all_to_all(array, "pcol", 0, 0, tiled=True)


def advect_kernel(u_ref, v_ref, dx_ref, yd_ref, out_ref):
    yd = yd_ref[...]
    for i in range(u_ref.shape[0]):
        u = u_ref[i]
        u_dy = jnp.dot(yd, u, preferred_element_type=F32)
        adv = u.astype(F32) * dx_ref[i].astype(F32) + v_ref[i].astype(F32) * u_dy
        out_ref[i] = adv.astype(out_ref.dtype)


def advection(u, v, dx, yd):
    z, y, x = u.shape
    zb = min(8, z)
    spec = pl.BlockSpec((zb, y, x), lambda i: (i, 0, 0))
    return pl.pallas_call(
        advect_kernel,
        grid=(z // zb,),
        out_shape=jax.ShapeDtypeStruct((z, y, x), BF16),
        in_specs=[spec, spec, spec, pl.BlockSpec((y, y), lambda i: (0, 0))],
        out_specs=spec,
        compiler_params=pltpu.CompilerParams(vmem_limit_bytes=32 * MIB),
        cost_estimate=pl.CostEstimate(flops=2 * z * y * y * x, bytes_accessed=8 * z * y * x, transcendentals=0),
        name="advection",
    )(u, v, dx, yd)


def div_kernel(v_ref, dx_ref, wdz_ref, yd_ref, out_ref):
    yd = yd_ref[...]
    for i in range(v_ref.shape[0]):
        v_dy = jnp.dot(yd, v_ref[i], preferred_element_type=F32)
        w_dz = wdz_ref[:, i].astype(F32).reshape(v_dy.shape)
        total = (dx_ref[i].astype(F32) + v_dy) + w_dz
        out_ref[i] = total.T


def divergence_of(v, dx, wdz, yd):
    z, y, x = v.shape
    parts, _, yl, _ = wdz.shape
    zb = min(8, z)
    spec = pl.BlockSpec((zb, y, x), lambda i: (i, 0, 0))
    wdz_spec = pl.BlockSpec((parts, zb, yl, x), lambda i: (0, i, 0, 0))
    return pl.pallas_call(
        div_kernel,
        grid=(z // zb,),
        out_shape=jax.ShapeDtypeStruct((z, x, y), F32),
        in_specs=[spec, spec, wdz_spec, pl.BlockSpec((y, y), lambda i: (0, 0))],
        out_specs=pl.BlockSpec((zb, x, y), lambda i: (i, 0, 0)),
        compiler_params=pltpu.CompilerParams(vmem_limit_bytes=32 * MIB),
        cost_estimate=pl.CostEstimate(flops=2 * z * y * y * x, bytes_accessed=10 * z * y * x, transcendentals=0),
        name="divergence",
    )(v, dx, wdz, yd)


def slope_kernel(w_ref, zd_ref, out_ref):
    parts, _, z, x = w_ref.shape
    w = w_ref[...].reshape(parts * z, x)
    slope = jnp.dot(zd_ref[...], w, preferred_element_type=F32)
    out_ref[...] = slope.astype(out_ref.dtype).reshape(out_ref.shape)


def z_slope(w, zd):
    parts, y, z, x = w.shape
    spec = pl.BlockSpec((parts, 1, z, x), lambda i: (0, i, 0, 0))
    full = parts * z
    return pl.pallas_call(
        slope_kernel,
        grid=(y,),
        out_shape=jax.ShapeDtypeStruct(w.shape, BF16),
        in_specs=[spec, pl.BlockSpec((full, full), lambda i: (0, 0))],
        out_specs=spec,
        compiler_params=pltpu.CompilerParams(vmem_limit_bytes=40 * MIB),
        cost_estimate=pl.CostEstimate(flops=2 * y * full * full * x, bytes_accessed=4 * y * full * x, transcendentals=0),
        name="z_slope",
    )(w, zd)


def tendency_kernel(u_ref, w_ref, adv_ref, zd_ref, out_ref):
    parts, _, z, x = w_ref.shape
    u = u_ref[...].reshape(parts * z, x)
    for c in range(parts):
        slope = jnp.dot(zd_ref[c * z:(c + 1) * z, :], u, preferred_element_type=F32)
        total = -(adv_ref[c, 0].astype(F32) + w_ref[c, 0].astype(F32) * slope)
        out_ref[0, :, c * z:(c + 1) * z] = total.T


def tendency(u, w, adv, zd):
    parts, y, z, x = w.shape
    spec = pl.BlockSpec((parts, 1, z, x), lambda i: (0, i, 0, 0))
    full = parts * z
    return pl.pallas_call(
        tendency_kernel,
        grid=(y,),
        out_shape=jax.ShapeDtypeStruct((y, x, full), F32),
        in_specs=[spec, spec, spec, pl.BlockSpec((full, full), lambda i: (0, 0))],
        out_specs=pl.BlockSpec((1, x, full), lambda i: (i, 0, 0)),
        compiler_params=pltpu.CompilerParams(vmem_limit_bytes=40 * MIB),
        cost_estimate=pl.CostEstimate(flops=2 * y * full * full * x, bytes_accessed=10 * y * full * x, transcendentals=0),
        name="tendency",
    )(u, w, adv, zd)


def after(array, *earlier):
    return lax.optimization_barrier((array, *earlier))[0]


def body(rows, cols, u, v, w, x_derivative, yd, z_derivative):
    y, z, x = u.shape
    xl, yl = x // rows, rows * y // cols
    y_full = rows * y
    plain = xl % 128 != 0 or z % 128 != 0

    (w_y,) = turn([w], rows, 0)
    xd = lax.all_gather(x_derivative, "pcol", axis=0, tiled=True)
    zd = lax.all_gather(z_derivative, "prow", axis=0, tiled=True)
    w_z = exchange(w_y.reshape(cols, yl, z, xl))

    u_y, v_y = turn([after(u, w_y), v], rows, 1)
    u_dx = lax.dot_general(
        u.reshape(y * z, x), xd, (((1,), (1,)), ((), ())), preferred_element_type=F32
    ).astype(BF16).reshape(y, z, x)
    (dx_y,) = turn([after(u_dx, v_y)], rows, 2)

    u_z = exchange(after(u_y, w_z).reshape(cols, yl, z, xl))
    u_t, v_t, dx_t = (jnp.transpose(a, (1, 0, 2)) for a in (u_y, v_y, dx_y))
    if plain:
        w_dz = jnp.einsum(
            "ak,kyx->ayx", zd, jnp.transpose(w_z, (0, 2, 1, 3)).reshape(cols * z, yl, xl), preferred_element_type=F32
        )
        w_dz = w_dz.astype(BF16).reshape(cols, z, yl, xl)
        u_dy = jnp.einsum("ab,zbx->zax", yd, u_t, preferred_element_type=F32)
        adv_t = (u_t.astype(F32) * dx_t.astype(F32) + v_t.astype(F32) * u_dy).astype(BF16)
    else:
        w_dz = jnp.transpose(z_slope(w_z, zd), (0, 2, 1, 3))
        adv_t = advection(u_t, v_t, dx_t, yd)
    wdz_y = exchange(after(w_dz, u_z))
    adv_y = jnp.transpose(adv_t, (1, 0, 2)).reshape(cols, yl, z, xl)
    adv_z = exchange(after(adv_y, wdz_y))
    if plain:
        wdz_t = jnp.transpose(wdz_y, (1, 0, 2, 3)).reshape(z, y_full, xl)
        v_dy = jnp.einsum("ab,zbx->zax", yd, v_t, preferred_element_type=F32)
        divergence = jnp.transpose(dx_t.astype(F32) + v_dy + wdz_t.astype(F32), (0, 2, 1))
        u_line, w_line, adv_line = (
            jnp.transpose(a, (1, 3, 0, 2)).reshape(yl, xl, cols * z) for a in (u_z, w_z, adv_z)
        )
        u_dz = jnp.einsum("ak,yxk->yxa", zd, u_line, preferred_element_type=F32)
        u_tendency = -(adv_line.astype(F32) + w_line.astype(F32) * u_dz)
    else:
        divergence = divergence_of(v_t, dx_t, wdz_y, yd)
        u_tendency = tendency(u_z, w_z, adv_z, zd)
    return u_tendency, divergence


def solution(mesh):
    in_specs = (
        P("prow", "pcol", None),
        P("prow", "pcol", None),
        P("prow", "pcol", None),
        P("pcol", None),
        P(),
        P("prow", None),
    )
    out_specs = (P("pcol", "prow", None), P("pcol", "prow", None))
    step = functools.partial(body, mesh.shape["prow"], mesh.shape["pcol"])
    return jax.shard_map(step, mesh=mesh, in_specs=in_specs, out_specs=out_specs, check_vma=False)
```

```python
import functools
import jax
import jax.numpy as jnp
from jax import lax
from jax.experimental import pallas as pl
from jax.experimental.pallas import tpu as pltpu
from jax.sharding import PartitionSpec as P

F32 = jnp.float32
BF16 = jnp.bfloat16
MIB = 1 << 20


def turn_kernel(rows, ready, *refs):
    count = (len(refs) - 3 - ready) // 2
    srcs, dsts = refs[:count], refs[count + ready:2 * count + ready]
    send_sem, recv_sem, own_sem = refs[2 * count + ready:]
    me = lax.axis_index("prow")
    barrier = pltpu.get_barrier_semaphore()
    for k in range(1, rows):
        pl.semaphore_signal(
            barrier, inc=1, device_id={"prow": lax.rem(me + k, rows)}, device_id_type=pl.DeviceIdType.MESH
        )
    pl.semaphore_wait(barrier, rows - 1)

    copies = []
    for n, (src, dst) in enumerate(zip(srcs, dsts)):
        width = dst.shape[-1]

        def columns(q):
            return src.at[:, :, pl.ds(pl.multiple_of(q * width, width), width)]

        for k in range(1, rows):
            q = lax.rem(me + k, rows)
            copy = pltpu.make_async_remote_copy(
                src_ref=columns(q),
                dst_ref=dst.at[me],
                send_sem=send_sem.at[n, k],
                recv_sem=recv_sem.at[n, k],
                device_id={"prow": q},
                device_id_type=pl.DeviceIdType.MESH,
            )
            copy.start()
            copies.append(copy)
        own = pltpu.make_async_copy(columns(me), dst.at[me], own_sem.at[n])
        own.start()
        copies.append(own)
    for copy in copies:
        copy.wait()


def turn(arrays, rows, number, ready=()):
    y, z, x = arrays[0].shape
    width = x // rows
    if width % 128:
        sent = [a.reshape(y, z, rows, width).transpose(2, 0, 1, 3) for a in arrays]
        return [lax.all_to_all(a, "prow", 0, 0, tiled=True).reshape(rows * y, z, width) for a in sent]
    count = len(arrays)
    outs = pl.pallas_call(
        functools.partial(turn_kernel, rows, len(ready)),
        out_shape=[jax.ShapeDtypeStruct((rows, y, z, width), a.dtype) for a in arrays],
        in_specs=[pl.BlockSpec(memory_space=pl.ANY)] * (count + len(ready)),
        out_specs=[pl.BlockSpec(memory_space=pl.ANY)] * count,
        scratch_shapes=[
            pltpu.SemaphoreType.DMA((count, rows)),
            pltpu.SemaphoreType.DMA((count, rows)),
            pltpu.SemaphoreType.DMA((count,)),
        ],
        compiler_params=pltpu.CompilerParams(collective_id=number, has_side_effects=True),
        cost_estimate=pl.CostEstimate(flops=0, bytes_accessed=250 * MIB * count, transcendentals=0),
        name=f"turn_{number}",
    )(*arrays, *ready)
    return [out.reshape(rows * y, z, width) for out in outs]


def exchange(array):
    return lax.all_to_all(array, "pcol", 0, 0, tiled=True)


def advect_kernel(u_ref, v_ref, dx_ref, yd_ref, out_ref):
    yd = yd_ref[...]
    for i in range(u_ref.shape[0]):
        u = u_ref[i]
        u_dy = jnp.dot(yd, u, preferred_element_type=F32)
        adv = u.astype(F32) * dx_ref[i].astype(F32) + v_ref[i].astype(F32) * u_dy
        out_ref[i] = adv.astype(out_ref.dtype)


def advection(u, v, dx, yd):
    z, y, x = u.shape
    zb = min(8, z)
    spec = pl.BlockSpec((zb, y, x), lambda i: (i, 0, 0))
    return pl.pallas_call(
        advect_kernel,
        grid=(z // zb,),
        out_shape=jax.ShapeDtypeStruct((z, y, x), BF16),
        in_specs=[spec, spec, spec, pl.BlockSpec((y, y), lambda i: (0, 0))],
        out_specs=spec,
        compiler_params=pltpu.CompilerParams(vmem_limit_bytes=32 * MIB),
        cost_estimate=pl.CostEstimate(flops=2 * z * y * y * x, bytes_accessed=8 * z * y * x, transcendentals=0),
        name="advection",
    )(u, v, dx, yd)


def div_kernel(v_ref, dx_ref, wdz_ref, yd_ref, out_ref):
    yd = yd_ref[...]
    for i in range(v_ref.shape[0]):
        v_dy = jnp.dot(yd, v_ref[i], preferred_element_type=F32)
        w_dz = wdz_ref[:, i].astype(F32).reshape(v_dy.shape)
        total = (dx_ref[i].astype(F32) + v_dy) + w_dz
        out_ref[i] = total.T


def divergence_of(v, dx, wdz, yd):
    z, y, x = v.shape
    parts, _, yl, _ = wdz.shape
    zb = min(8, z)
    spec = pl.BlockSpec((zb, y, x), lambda i: (i, 0, 0))
    wdz_spec = pl.BlockSpec((parts, zb, yl, x), lambda i: (0, i, 0, 0))
    return pl.pallas_call(
        div_kernel,
        grid=(z // zb,),
        out_shape=jax.ShapeDtypeStruct((z, x, y), F32),
        in_specs=[spec, spec, wdz_spec, pl.BlockSpec((y, y), lambda i: (0, 0))],
        out_specs=pl.BlockSpec((zb, x, y), lambda i: (i, 0, 0)),
        compiler_params=pltpu.CompilerParams(vmem_limit_bytes=32 * MIB),
        cost_estimate=pl.CostEstimate(flops=2 * z * y * y * x, bytes_accessed=10 * z * y * x, transcendentals=0),
        name="divergence",
    )(v, dx, wdz, yd)


def slope_kernel(w_ref, zd_ref, _, out_ref):
    parts, _, z, x = w_ref.shape
    w = w_ref[...].reshape(parts * z, x)
    slope = jnp.dot(zd_ref[...], w, preferred_element_type=F32)
    out_ref[...] = slope.astype(out_ref.dtype).reshape(out_ref.shape)


def z_slope(w, zd, ready):
    parts, y, z, x = w.shape
    spec = pl.BlockSpec((parts, 1, z, x), lambda i: (0, i, 0, 0))
    full = parts * z
    return pl.pallas_call(
        slope_kernel,
        grid=(y,),
        out_shape=jax.ShapeDtypeStruct(w.shape, BF16),
        in_specs=[spec, pl.BlockSpec((full, full), lambda i: (0, 0)), pl.BlockSpec(memory_space=pl.ANY)],
        out_specs=spec,
        compiler_params=pltpu.CompilerParams(vmem_limit_bytes=40 * MIB),
        cost_estimate=pl.CostEstimate(flops=2 * y * full * full * x, bytes_accessed=4 * y * full * x, transcendentals=0),
        name="z_slope",
    )(w, zd, ready)


def tendency_kernel(u_ref, w_ref, adv_ref, zd_ref, out_ref):
    parts, _, z, x = w_ref.shape
    u = u_ref[...].reshape(parts * z, x)
    for c in range(parts):
        slope = jnp.dot(zd_ref[c * z:(c + 1) * z, :], u, preferred_element_type=F32)
        total = -(adv_ref[c, 0].astype(F32) + w_ref[c, 0].astype(F32) * slope)
        out_ref[0, :, c * z:(c + 1) * z] = total.T


def tendency(u, w, adv, zd):
    parts, y, z, x = w.shape
    spec = pl.BlockSpec((parts, 1, z, x), lambda i: (0, i, 0, 0))
    full = parts * z
    return pl.pallas_call(
        tendency_kernel,
        grid=(y,),
        out_shape=jax.ShapeDtypeStruct((y, x, full), F32),
        in_specs=[spec, spec, spec, pl.BlockSpec((full, full), lambda i: (0, 0))],
        out_specs=pl.BlockSpec((1, x, full), lambda i: (i, 0, 0)),
        compiler_params=pltpu.CompilerParams(vmem_limit_bytes=40 * MIB),
        cost_estimate=pl.CostEstimate(flops=2 * y * full * full * x, bytes_accessed=10 * y * full * x, transcendentals=0),
        name="tendency",
    )(u, w, adv, zd)


def after(array, *earlier):
    return lax.optimization_barrier((array, *earlier))[0]


def body(rows, cols, u, v, w, x_derivative, yd, z_derivative):
    y, z, x = u.shape
    xl, yl = x // rows, rows * y // cols
    y_full = rows * y
    plain = xl % 128 != 0 or z % 128 != 0

    xd = lax.all_gather(x_derivative, "pcol", axis=0, tiled=True)
    (w_y,) = turn([w], rows, 0, [xd])
    zd = lax.all_gather(z_derivative, "prow", axis=0, tiled=True)
    w_z = exchange(w_y.reshape(cols, yl, z, xl))

    u_y, v_y = turn([after(u, w_y), v], rows, 1)
    u_dx = lax.dot_general(
        u.reshape(y * z, x), xd, (((1,), (1,)), ((), ())), preferred_element_type=F32
    ).astype(BF16).reshape(y, z, x)
    (dx_y,) = turn([after(u_dx, v_y)], rows, 2)

    u_z = exchange(after(u_y, w_z).reshape(cols, yl, z, xl))
    u_t, v_t, dx_t = (jnp.transpose(a, (1, 0, 2)) for a in (u_y, v_y, dx_y))
    if plain:
        w_dz = jnp.einsum(
            "ak,kyx->ayx", zd, jnp.transpose(w_z, (0, 2, 1, 3)).reshape(cols * z, yl, xl), preferred_element_type=F32
        )
        w_dz = w_dz.astype(BF16).reshape(cols, z, yl, xl)
        u_dy = jnp.einsum("ab,zbx->zax", yd, u_t, preferred_element_type=F32)
        adv_t = (u_t.astype(F32) * dx_t.astype(F32) + v_t.astype(F32) * u_dy).astype(BF16)
    else:
        w_dz = jnp.transpose(z_slope(w_z, zd, v_y), (0, 2, 1, 3))
        adv_t = advection(u_t, v_t, dx_t, yd)
    wdz_y = exchange(after(w_dz, u_z))
    adv_y = jnp.transpose(adv_t, (1, 0, 2)).reshape(cols, yl, z, xl)
    adv_z = exchange(after(adv_y, wdz_y))
    if plain:
        wdz_t = jnp.transpose(wdz_y, (1, 0, 2, 3)).reshape(z, y_full, xl)
        v_dy = jnp.einsum("ab,zbx->zax", yd, v_t, preferred_element_type=F32)
        divergence = jnp.transpose(dx_t.astype(F32) + v_dy + wdz_t.astype(F32), (0, 2, 1))
        u_line, w_line, adv_line = (
            jnp.transpose(a, (1, 3, 0, 2)).reshape(yl, xl, cols * z) for a in (u_z, w_z, adv_z)
        )
        u_dz = jnp.einsum("ak,yxk->yxa", zd, u_line, preferred_element_type=F32)
        u_tendency = -(adv_line.astype(F32) + w_line.astype(F32) * u_dz)
    else:
        divergence = divergence_of(v_t, dx_t, wdz_y, yd)
        u_tendency = tendency(u_z, w_z, adv_z, zd)
    return u_tendency, divergence


def solution(mesh):
    in_specs = (
        P("prow", "pcol", None),
        P("prow", "pcol", None),
        P("prow", "pcol", None),
        P("pcol", None),
        P(),
        P("prow", None),
    )
    out_specs = (P("pcol", "prow", None), P("pcol", "prow", None))
    step = functools.partial(body, mesh.shape["prow"], mesh.shape["pcol"])
    return jax.shard_map(step, mesh=mesh, in_specs=in_specs, out_specs=out_specs, check_vma=False)
```
